32 devices in a mesh: aux: 16 (over z, y, x), occ: 2 (over core).
Axes of the slice: x: 2, y: 2, z: 4, core: 2. Of those that a mesh axis runs over, the one named last changes fastest.
Arguments:
- three_index: bfloat16 [64, 64, 64, 128], P('aux'), may hold values from -0.29882812 to 0.29882812
- coefficients: bfloat16 [5120, 256], P('aux', 'occ'), may hold values from -0.5 to 0.5
- row_blocks: int32 [64], P('aux'), may hold values from 0 to 15, as said below
- basis_blocks: int32 [64, 2], P('aux'), may hold values from 0 to 79, as said below
- fock_slot: int32 [112], replicated, may hold values from 0 to 111, as said below
Outputs:
- exchange: float32 [112, 4096], P('aux', 'occ')
The draws below stay inside these ranges and needn't reach their ends.
Inputs may be any that keep to these rules, and one draw needn't show every extreme that they name: There is one offset c, the same for row_blocks and fock_slot: the 4 row blocks of aux index a are (a + c + s_j) mod 16 for j = 0..3, in order, with s_j = j * 4 for j < 3 and s_j = 15 for the last. `basis_blocks`: aux index a lists only basis blocks held by aux indices a - 1, a and a + 1 (cyclically, 5 blocks each, block b held by index b // 5); every aux index lists some block of a - 1 and some of a + 1. `fock_slot`: each position once; the 7 band blocks of row block r go, in some order, to positions ((r - c) mod 16) * 7 to ((r - c) mod 16) * 7 + 6, with the c of row_blocks.
All inputs are finite; a program needn't handle non-finite values.
Results may differ from the reference program's by a relative error of at most 0.00034.
Values may be sent and summed in bfloat16 or wider, within the bound.
No kernel may reach another device: no remote copies, remote signals or barrier semaphores. Data moves between devices by JAX's collectives and lax.ppermute only.
A program may use at most 64 MiB of HBM per device.

```python
import jax
import jax.numpy as jnp
from jax import lax

BLOCK = 64
AUX_DEV = 64
BASIS_DEV = 5
ROWBLK = 4
TILES_ROW = 2
OCC = 256
NBF = 5120
WINDOW = 16
BAND = 7
FOCK = 112
N_AUX = 16


def common_offset(key):
    return jax.random.randint(jax.random.fold_in(key, 21), (), 0, WINDOW)


def draw_row_blocks(key, part):
    offset = common_offset(key)
    steps = jnp.arange(ROWBLK) * WINDOW // ROWBLK
    steps = steps.at[ROWBLK - 1].set(WINDOW - 1)
    starts = (jnp.arange(N_AUX) + offset) % WINDOW
    listed = (starts[:, None] + steps[None, :]) % WINDOW
    return listed.reshape(-1).astype(jnp.int32)


def shuffle_row(row_key):
    return jax.random.permutation(row_key, ROWBLK * TILES_ROW)


def shuffle_band(row_key):
    return jax.random.permutation(row_key, BAND)


def draw_basis_blocks(key, part):
    count = ROWBLK * TILES_ROW
    key_side = jax.random.fold_in(key, 11)
    key_within = jax.random.fold_in(key, 12)
    key_order = jax.random.fold_in(key, 13)
    sides = jax.random.randint(key_side, (N_AUX, count), -1, 2)
    sides = sides.at[:, 0].set(-1).at[:, 1].set(1)
    orders = jax.vmap(shuffle_row)(jax.random.split(key_order, N_AUX))
    sides = jnp.take_along_axis(sides, orders, axis=1)
    within = jax.random.randint(key_within, (N_AUX, count), 0, BASIS_DEV)
    owner = (jnp.arange(N_AUX)[:, None] + sides) % N_AUX
    listed = owner * BASIS_DEV + within
    return listed.reshape(N_AUX * ROWBLK, TILES_ROW).astype(jnp.int32)


def draw_fock_slot(key, part):
    offset = common_offset(key)
    key_band = jax.random.fold_in(key, 22)
    orders = jax.vmap(shuffle_band)(jax.random.split(key_band, WINDOW))
    owner = (jnp.arange(WINDOW) - offset) % WINDOW
    listed = owner[:, None] * BAND + orders
    return listed.reshape(-1).astype(jnp.int32)


def levels(stream_key, dims, cuts, smallest, top_value):
    factor_of, own = 1.0, jax.random.fold_in(stream_key, 6)
    for position, shards_of in cuts:
        heights = jnp.exp(jax.random.uniform(jax.random.fold_in(own, position), (shards_of,), jnp.float32, smallest / len(cuts), top_value / len(cuts)))
        factor_of = factor_of * jnp.repeat(heights, dims[position] // shards_of).reshape([-1 if axis == position else 1 for axis in range(len(dims))])
    return factor_of


def noise(key, shape, spread, bound, cuts=(), kind=jnp.bfloat16):
    values = spread * jax.random.normal(key, shape, jnp.float32)
    if cuts:
        values = values * levels(key, shape, cuts, -0.22, 0.18)
    return jnp.clip(values, -bound, bound).astype(kind)


def setup_inputs(seed: int = 0) -> dict:
    arg_keys = jax.random.split(jax.random.key(seed), 6)
    three_index = noise(arg_keys[0], (N_AUX * ROWBLK, AUX_DEV, BLOCK, TILES_ROW * BLOCK), 0.05, 0.29882812, ((0, 16),))
    coefficients = noise(arg_keys[1], (NBF, OCC), (TILES_ROW * BLOCK) ** -0.5, 0.5, ((0, 16), (1, 2)))
    row_blocks = draw_row_blocks(jax.random.fold_in(arg_keys[5], 71), 0)
    basis_blocks = draw_basis_blocks(jax.random.fold_in(arg_keys[5], 71), 0)
    fock_slot = draw_fock_slot(jax.random.fold_in(arg_keys[5], 71), 0)
    return {"three_index": three_index, "coefficients": coefficients, "row_blocks": row_blocks, "basis_blocks": basis_blocks, "fock_slot": fock_slot}


def reference(three_index, coefficients, row_blocks, basis_blocks, fock_slot):
    band_width = 2 * ROWBLK - 1
    tile_lists = three_index.reshape(N_AUX, ROWBLK, AUX_DEV, BLOCK, TILES_ROW * BLOCK)
    row_lists = row_blocks.reshape(N_AUX, ROWBLK)
    basis_lists = basis_blocks.reshape(N_AUX, ROWBLK, TILES_ROW)
    entry_index = jnp.arange(ROWBLK, dtype=jnp.int32)
    offset_pair = entry_index[None, :] - entry_index[:, None] + ROWBLK - 1

    def pick_rows(block_id):
        start = (block_id * BLOCK).astype(jnp.int32)
        return lax.dynamic_slice_in_dim(coefficients, start, BLOCK, 0)

    def accumulate(fock_sums, inputs):
        tile_group, row_group, basis_group = inputs
        selected = jax.vmap(jax.vmap(pick_rows))(basis_group)
        selected = selected.reshape(ROWBLK, TILES_ROW * BLOCK, OCC)
        halfway = jnp.einsum("jpmk,jko->jpmo", tile_group.astype(jnp.float32), selected.astype(jnp.float32))
        halfway = halfway.astype(jnp.bfloat16).astype(jnp.float32)
        partial_value = jnp.einsum("jpmo,kpno->jkmn", halfway, halfway)
        partial_value = partial_value.reshape(ROWBLK * ROWBLK, BLOCK * BLOCK)
        band_index = (row_group[:, None] * band_width + offset_pair).reshape(-1).astype(jnp.int32)
        target = fock_slot[band_index]
        return fock_sums.at[target].add(partial_value), None

    fock_zero = jnp.zeros((FOCK, BLOCK * BLOCK), jnp.float32)
    fock_sums, _ = lax.scan(accumulate, fock_zero, (tile_lists, row_lists, basis_lists))
    return fock_sums
```

```python
import functools

import jax
import jax.numpy as jnp
from jax import lax
from jax.experimental import pallas as pl
from jax.experimental.pallas import tpu as pltpu
from jax.sharding import PartitionSpec as P

LANES = 128
CHUNK = 8
VMEM = pl.BlockSpec(memory_space=pltpu.VMEM)
SMEM = pl.BlockSpec(memory_space=pltpu.SMEM)


def build_kernel(groups, parts, blocks_ref, left_ref, own_ref, right_ref, three_ref, *rest):
    outs, (near, sel, half, acc, panels) = rest[:parts], rest[parts:]
    entries, aux_count, block, depth = three_ref.shape
    tiles = depth // block
    shard_rows, orbitals = own_ref.shape
    per_shard = shard_rows // block
    position = lax.axis_index("aux")
    lane = lax.axis_index("occ")

    near[0:shard_rows] = left_ref[...]
    near[shard_rows : 2 * shard_rows] = own_ref[...]
    near[2 * shard_rows : 3 * shard_rows] = right_ref[...]
    total = groups * per_shard
    for pair in range(entries // 2):
        sel[pair] = jnp.zeros(sel.shape[1:], sel.dtype)
    for e in range(entries):
        for t in range(tiles):
            offset = lax.rem(blocks_ref[e, t] - (position - 1) * per_shard + total, total)
            rows = near[pl.ds(pl.multiple_of(offset * block, block), block), :]
            at = (e % 2) * depth + t * block
            sel[e // 2, at : at + block, (e % 2) * orbitals : (e % 2 + 1) * orbitals] = rows

    acc[...] = jnp.zeros_like(acc)

    def step(s, carry):
        start = pl.multiple_of(s * CHUNK, CHUNK)
        for pair in range(entries // 2):
            lhs = jnp.concatenate(
                [three_ref[2 * pair + i, pl.ds(start, CHUNK)].reshape(CHUNK * block, depth) for i in range(2)], axis=1
            )
            res = jnp.dot(lhs, sel[pair], preferred_element_type=jnp.float32).astype(jnp.bfloat16)
            for i in range(2):
                e = 2 * pair + i
                for p in range(CHUNK):
                    half[e * block : (e + 1) * block, p * orbitals : (p + 1) * orbitals] = res[
                        p * block : (p + 1) * block, i * orbitals : (i + 1) * orbitals
                    ]
        full = half[...]
        acc[...] += lax.dot_general(full, full, (((1,), (1,)), ((), ())), preferred_element_type=jnp.float32)
        return carry

    lax.fori_loop(0, aux_count // CHUNK, step, 0)

    for h in range(entries // 2):
        panels[h] = acc[:, h * LANES : (h + 1) * LANES]
    count = block * block // parts // LANES
    low = lax.broadcasted_iota(jnp.int32, (count, LANES), 1) < block
    for r in range(parts):
        part = lax.rem(lane + r, parts)
        for j in range(entries):
            base = j * block + part * (block // parts)
            for k in range(0, entries, 2):
                even = panels[k // 2, pl.ds(base, count, stride=2), :]
                odd = panels[k // 2, pl.ds(base + 1, count, stride=2), :]
                outs[r][j, k] = jnp.where(low, even, pltpu.roll(odd, block, 1))
                outs[r][j, k + 1] = jnp.where(low, pltpu.roll(even, block, 1), odd)


def sum_kernel(parts, *refs):
    terms, outs = refs[:parts], refs[parts:]
    for j in range(len(outs)):
        value = terms[0][j]
        for term in terms[1:]:
            value = value + term[j]
        outs[j][...] = value


def place_kernel(slot_ref, row_ref, *refs):
    terms, out_ref, rows = refs[:-2], refs[-2], refs[-1]
    entries, _, count, _ = (len(terms),) + terms[0].shape
    band = 2 * entries - 1
    first = lax.axis_index("aux") * band
    row = row_ref[0] * band
    for off in range(band):
        value = None
        for j in range(entries):
            k = off - (entries - 1) + j
            if 0 <= k < entries:
                term = terms[j][k]
                value = term if value is None else value + term
        slot = slot_ref[row + off] - first
        rows[pl.ds(slot, count, stride=8), :] = value
    for c in range(count):
        out_ref[:, c * LANES : (c + 1) * LANES] = rows[c * 8 : c * 8 + band, :]


def per_device(three_index, coefficients, row_blocks, basis_blocks, fock_slot):
    entries, aux_count, block, depth = three_index.shape
    shard_rows, orbitals = coefficients.shape
    groups = lax.axis_size("aux")
    parts = lax.axis_size("occ")
    count = block * block // parts // LANES
    band = 2 * entries - 1

    def shift(value, axis, by):
        size = lax.axis_size(axis)
        return lax.ppermute(value, axis, [(i, (i + by) % size) for i in range(size)])

    left = shift(coefficients, "aux", 1)
    right = shift(coefficients, "aux", -1)
    pieces = pl.pallas_call(
        functools.partial(build_kernel, groups, parts),
        out_shape=[jax.ShapeDtypeStruct((entries, entries, count, LANES), jnp.float32)] * parts,
        in_specs=[SMEM, VMEM, VMEM, VMEM, VMEM],
        out_specs=[VMEM] * parts,
        scratch_shapes=[
            pltpu.VMEM((3 * shard_rows, orbitals), jnp.bfloat16),
            pltpu.VMEM((entries // 2, 2 * depth, 2 * orbitals), jnp.bfloat16),
            pltpu.VMEM((entries * block, CHUNK * orbitals), jnp.bfloat16),
            pltpu.VMEM((entries * block, entries * block), jnp.float32),
            pltpu.VMEM((entries // 2, entries * block, LANES), jnp.float32),
        ],
        compiler_params=pltpu.CompilerParams(vmem_limit_bytes=24 * 1024 * 1024),
    )(basis_blocks, left, coefficients, right, three_index)
    terms = [pieces[0]] + [shift(pieces[r], "occ", r) for r in range(1, parts)]
    rows = pl.pallas_call(
        functools.partial(sum_kernel, parts),
        out_shape=[jax.ShapeDtypeStruct((entries, count, LANES), jnp.float32)] * entries,
        in_specs=[VMEM] * parts,
        out_specs=[VMEM] * entries,
        compiler_params=pltpu.CompilerParams(vmem_limit_bytes=4 * 1024 * 1024),
    )(*terms)
    steps = [j * groups // entries for j in range(entries - 1)] + [groups - 1]
    moved = [rows[0]] + [shift(rows[j], "aux", steps[j]) for j in range(1, entries)]
    return pl.pallas_call(
        place_kernel,
        out_shape=jax.ShapeDtypeStruct((band, count * LANES), jnp.float32),
        in_specs=[SMEM, SMEM] + [VMEM] * entries,
        out_specs=VMEM,
        scratch_shapes=[pltpu.VMEM((count * 8, LANES), jnp.float32)],
        compiler_params=pltpu.CompilerParams(vmem_limit_bytes=4 * 1024 * 1024),
    )(fock_slot, row_blocks, *moved)


def solution(mesh):
    in_specs = (P("aux", None, None, None), P("aux", "occ"), P("aux"), P("aux", None), P())
    out_specs = P("aux", "occ")
    return jax.shard_map(
        per_device, mesh=mesh, in_specs=in_specs, out_specs=out_specs, check_vma=False
    )
```

```python
import functools

import jax
import jax.numpy as jnp
from jax import lax
from jax.experimental import pallas as pl
from jax.experimental.pallas import tpu as pltpu
from jax.sharding import PartitionSpec as P

LANES = 128
CHUNK = 16
VMEM = pl.BlockSpec(memory_space=pltpu.VMEM)
SMEM = pl.BlockSpec(memory_space=pltpu.SMEM)


def fetch_kernel(source, target, sem):
    copy = pltpu.make_async_copy(source, target, sem)
    copy.start()
    copy.wait()


def build_kernel(groups, parts, blocks_ref, far_ref, own_ref, near_ref, three_ref, *rest):
    outs, (near, sel, half, acc, panels) = rest[:parts], rest[parts:]
    entries, aux_count, block, depth = three_ref.shape
    tiles = depth // block
    shard_rows, orbitals = own_ref.shape
    per_shard = shard_rows // block
    position = lax.axis_index("aux")
    lane = lax.axis_index("occ")

    offset = lax.rem(blocks_ref[...] - (position - 1) * per_shard + groups * per_shard, groups * per_shard)
    side, within = lax.div(offset, per_shard), lax.rem(offset, per_shard)
    offsets = (jnp.where(lax.rem(position, 2) == 0, side, 2 - side) * per_shard + within).astype(jnp.float32)
    tile_at = lax.broadcasted_iota(jnp.int32, offsets.shape, 0)
    entry_at = lax.broadcasted_iota(jnp.int32, offsets.shape, 1)

    near[0:shard_rows] = far_ref[...]
    near[shard_rows : 2 * shard_rows] = own_ref[...]
    near[2 * shard_rows : 3 * shard_rows] = near_ref[...]
    for pair in range(entries // 2):
        sel[pair] = jnp.zeros(sel.shape[1:], sel.dtype)
    for e in range(entries):
        for t in range(tiles):
            mine = (tile_at == t) & (entry_at == e)
            offset = jnp.max(jnp.where(mine, offsets, 0.0)).astype(jnp.int32) * block
            rows = near[pl.ds(pl.multiple_of(offset, block), block), :]
            at = (e % 2) * depth + t * block
            sel[e // 2, at : at + block, (e % 2) * orbitals : (e % 2 + 1) * orbitals] = rows

    acc[...] = jnp.zeros_like(acc)

    def step(s, carry):
        start = pl.multiple_of(s * CHUNK, CHUNK)
        for pair in range(entries // 2):
            lhs = jnp.concatenate(
                [three_ref[2 * pair + i, pl.ds(start, CHUNK)].reshape(CHUNK * block, depth) for i in range(2)], axis=1
            )
            res = jnp.dot(lhs, sel[pair], preferred_element_type=jnp.float32).astype(jnp.bfloat16)
            for i in range(2):
                e = 2 * pair + i
                for p in range(CHUNK):
                    half[e * block : (e + 1) * block, p * orbitals : (p + 1) * orbitals] = res[
                        p * block : (p + 1) * block, i * orbitals : (i + 1) * orbitals
                    ]
        full = half[...]
        acc[...] += lax.dot_general(full, full, (((1,), (1,)), ((), ())), preferred_element_type=jnp.float32)
        return carry

    lax.fori_loop(0, aux_count // CHUNK, step, 0, unroll=True)

    for h in range(entries // 2):
        panels[h] = acc[:, h * LANES : (h + 1) * LANES]
    count = block * block // parts // LANES
    low = lax.broadcasted_iota(jnp.int32, (count, LANES), 1) < block
    for r in range(parts):
        part = lax.rem(lane + r, parts)
        for j in range(entries):
            base = j * block + part * (block // parts)
            for k in range(0, entries, 2):
                even = panels[k // 2, pl.ds(base, count, stride=2), :]
                odd = panels[k // 2, pl.ds(base + 1, count, stride=2), :]
                outs[r][j, k] = jnp.where(low, even, pltpu.roll(odd, block, 1))
                outs[r][j, k + 1] = jnp.where(low, pltpu.roll(even, block, 1), odd)


def sum_kernel(parts, *refs):
    terms, outs = refs[:parts], refs[parts:]
    for j in range(len(outs)):
        value = terms[0][j]
        for term in terms[1:]:
            value = value + term[j]
        outs[j][...] = value


def place_kernel(slot_ref, *refs):
    terms, out_ref, rows = refs[:-2], refs[-2], refs[-1]
    entries, count = len(terms), terms[0].shape[1]
    band = 2 * entries - 1
    for off in range(band):
        value = None
        for j in range(entries):
            k = off - (entries - 1) + j
            if 0 <= k < entries:
                term = terms[j][k]
                value = term if value is None else value + term
        rows[pl.ds(off, count, stride=8), :] = value
    shape = (8, slot_ref.shape[1])
    lines = lax.broadcasted_iota(jnp.int32, shape, 0) + lax.axis_index("aux") * band
    offs = lax.rem(lax.broadcasted_iota(jnp.int32, shape, 1), band).astype(jnp.float32)
    order = jnp.sum(jnp.where(slot_ref[...] == lines, offs, 0.0), axis=1, keepdims=True).astype(jnp.int32)
    order = jnp.broadcast_to(jnp.minimum(order, 7), (8, LANES))
    for c in range(count):
        placed = jnp.take_along_axis(rows[c * 8 : c * 8 + 8, :], order, axis=0, mode="promise_in_bounds")
        out_ref[:, c * LANES : (c + 1) * LANES] = placed[:band]


def per_device(three_index, coefficients, row_blocks, basis_blocks, fock_slot):
    entries, aux_count, block, depth = three_index.shape
    shard_rows, orbitals = coefficients.shape
    groups = lax.axis_size("aux")
    parts = lax.axis_size("occ")
    count = block * block // parts // LANES
    band = 2 * entries - 1

    def shift(value, axis, by):
        size = lax.axis_size(axis)
        return lax.ppermute(value, axis, [(i, (i + by) % size) for i in range(size)])

    def swap(value, first):
        pairs = [((i + first) % groups, (i + first + 1) % groups) for i in range(0, groups, 2)]
        return lax.ppermute(value, "aux", pairs + [(b, a) for a, b in pairs])

    neighbour = swap(coefficients, 0)
    other = swap(coefficients, 1)
    held = pl.pallas_call(
        fetch_kernel,
        out_shape=jax.ShapeDtypeStruct(three_index.shape, three_index.dtype),
        in_specs=[pl.BlockSpec(memory_space=pl.ANY)],
        out_specs=VMEM,
        scratch_shapes=[pltpu.SemaphoreType.DMA],
        compiler_params=pltpu.CompilerParams(vmem_limit_bytes=8 * 1024 * 1024),
    )(three_index)
    pieces = pl.pallas_call(
        functools.partial(build_kernel, groups, parts),
        out_shape=[jax.ShapeDtypeStruct((entries, entries, count, LANES), jnp.float32)] * parts,
        in_specs=[VMEM] * 5,
        out_specs=[VMEM] * parts,
        scratch_shapes=[
            pltpu.VMEM((3 * shard_rows, orbitals), jnp.bfloat16),
            pltpu.VMEM((entries // 2, 2 * depth, 2 * orbitals), jnp.bfloat16),
            pltpu.VMEM((entries * block, CHUNK * orbitals), jnp.bfloat16),
            pltpu.VMEM((entries * block, entries * block), jnp.float32),
            pltpu.VMEM((entries // 2, entries * block, LANES), jnp.float32),
        ],
        compiler_params=pltpu.CompilerParams(vmem_limit_bytes=12 * 1024 * 1024),
    )(basis_blocks.T, other, coefficients, neighbour, held)
    terms = [pieces[0]] + [shift(pieces[r], "occ", r) for r in range(1, parts)]
    rows = pl.pallas_call(
        functools.partial(sum_kernel, parts),
        out_shape=[jax.ShapeDtypeStruct((entries, count, LANES), jnp.float32)] * entries,
        in_specs=[VMEM] * parts,
        out_specs=[VMEM] * entries,
        compiler_params=pltpu.CompilerParams(vmem_limit_bytes=4 * 1024 * 1024),
    )(*terms)
    steps = [j * groups // entries for j in range(entries - 1)] + [groups - 1]
    moved = [rows[0]] + [shift(rows[j], "aux", steps[j]) for j in range(1, entries)]
    return pl.pallas_call(
        place_kernel,
        out_shape=jax.ShapeDtypeStruct((band, count * LANES), jnp.float32),
        in_specs=[VMEM] * (entries + 1),
        out_specs=VMEM,
        scratch_shapes=[pltpu.VMEM((count * 8, LANES), jnp.float32)],
        compiler_params=pltpu.CompilerParams(vmem_limit_bytes=4 * 1024 * 1024),
    )(fock_slot.reshape(1, -1), *moved)


def solution(mesh):
    in_specs = (P("aux", None, None, None), P("aux", "occ"), P("aux"), P("aux", None), P())
    out_specs = P("aux", "occ")
    return jax.shard_map(
        per_device, mesh=mesh, in_specs=in_specs, out_specs=out_specs, check_vma=False
    )
```

```python
import functools

import jax
import jax.numpy as jnp
from jax import lax
from jax.experimental import pallas as pl
from jax.experimental.pallas import tpu as pltpu
from jax.sharding import PartitionSpec as P

LANES = 128
ROUTES = {
    16: [
        [8, 9, 10, 2, 12, 4, 5, 11, 7, 13, 14, 15, 0, 1, 6, 3],
        [4, 5, 6, 7, 8, 13, 10, 15, 0, 1, 9, 3, 11, 12, 2, 14],
        [15, 0, 1, 11, 3, 9, 14, 6, 12, 8, 2, 10, 4, 5, 13, 7],
    ],
}
CHUNK = 8
VMEM = pl.BlockSpec(memory_space=pltpu.VMEM)
SMEM = pl.BlockSpec(memory_space=pltpu.SMEM)


def fetch_kernel(source, target, sem):
    copy = pltpu.make_async_copy(source, target, sem)
    copy.start()
    copy.wait()


def build_kernel(groups, parts, blocks_ref, near_ref, own_ref, far_ref, three_ref, *rest):
    outs, (near, sel, half, acc, panels) = rest[:parts], rest[parts:]
    entries, aux_count, block, depth = three_ref.shape
    tiles = depth // block
    shard_rows, orbitals = own_ref.shape
    per_shard = shard_rows // block
    position = lax.axis_index("aux")
    lane = lax.axis_index("occ")

    offset = lax.rem(blocks_ref[...] - (position - 1) * per_shard + groups * per_shard, groups * per_shard)
    side, within = lax.div(offset, per_shard), lax.rem(offset, per_shard)
    offsets = ((2 - side) * per_shard + within).astype(jnp.float32)
    tile_at = lax.broadcasted_iota(jnp.int32, offsets.shape, 0)
    entry_at = lax.broadcasted_iota(jnp.int32, offsets.shape, 1)

    near[0:shard_rows] = far_ref[...]
    near[shard_rows : 2 * shard_rows] = own_ref[...]
    near[2 * shard_rows : 3 * shard_rows] = near_ref[...]
    for pair in range(entries // 2):
        sel[pair] = jnp.zeros(sel.shape[1:], sel.dtype)
    for e in range(entries):
        for t in range(tiles):
            mine = (tile_at == t) & (entry_at == e)
            offset = jnp.max(jnp.where(mine, offsets, 0.0)).astype(jnp.int32) * block
            rows = near[pl.ds(pl.multiple_of(offset, block), block), :]
            at = (e % 2) * depth + t * block
            sel[e // 2, at : at + block, (e % 2) * orbitals : (e % 2 + 1) * orbitals] = rows

    acc[...] = jnp.zeros_like(acc)

    def step(s, carry):
        start = pl.multiple_of(s * CHUNK, CHUNK)
        for pair in range(entries // 2):
            lhs = jnp.concatenate(
                [three_ref[2 * pair + i, pl.ds(start, CHUNK)].reshape(CHUNK * block, depth) for i in range(2)], axis=1
            )
            res = jnp.dot(lhs, sel[pair], preferred_element_type=jnp.float32).astype(jnp.bfloat16)
            for i in range(2):
                e = 2 * pair + i
                for p in range(CHUNK):
                    half[e * block : (e + 1) * block, p * orbitals : (p + 1) * orbitals] = res[
                        p * block : (p + 1) * block, i * orbitals : (i + 1) * orbitals
                    ]
        full = half[...]
        acc[...] += lax.dot_general(full, full, (((1,), (1,)), ((), ())), preferred_element_type=jnp.float32)
        return carry

    lax.fori_loop(0, aux_count // CHUNK, step, 0, unroll=True)

    for h in range(entries // 2):
        panels[h] = acc[:, h * LANES : (h + 1) * LANES]
    count = block * block // parts // LANES
    low = lax.broadcasted_iota(jnp.int32, (count, LANES), 1) < block
    for r in range(parts):
        part = lax.rem(lane + r, parts)
        for j in range(entries):
            base = j * block + part * (block // parts)
            for k in range(0, entries, 2):
                even = panels[k // 2, pl.ds(base, count, stride=2), :]
                odd = panels[k // 2, pl.ds(base + 1, count, stride=2), :]
                outs[r][j, k] = jnp.where(low, even, pltpu.roll(odd, block, 1))
                outs[r][j, k + 1] = jnp.where(low, pltpu.roll(even, block, 1), odd)


def route(groups, entries):
    steps = [j * groups // entries for j in range(entries - 1)] + [groups - 1]
    targets = ROUTES.get(groups) or [[(i + step) % groups for i in range(groups)] for step in steps[1:]]
    sends = [[steps.index((t - i) % groups) for i, t in enumerate(each)] for each in targets]
    takes = [[sent[each.index(i)] for i in range(groups)] for each, sent in zip(targets, sends)]
    return targets, sends, takes


def entry_of(table, position):
    if len(set(table)) == 1:
        return table[0]
    packed = sum(value << (2 * i) for i, value in enumerate(table))
    packed = jnp.int32(packed - (1 << 32) if packed >= 1 << 31 else packed)
    return lax.shift_right_logical(packed, 2 * position) & 3


def sum_kernel(parts, sends, *refs):
    terms, outs = refs[:parts], refs[parts:]
    position = lax.axis_index("aux")
    for out, table in zip(outs, [[0]] + sends):
        j = entry_of(table, position)
        value = terms[0][j]
        for term in terms[1:]:
            value = value + term[j]
        out[...] = value


def place_kernel(takes, slot_ref, *refs):
    terms, out_ref, rows = refs[:-2], refs[-2], refs[-1]
    position = lax.axis_index("aux")
    entries, count = len(terms), terms[0].shape[1]
    band = 2 * entries - 1
    given = [entry_of(table, position) for table in takes]

    def term_of(j, k):
        if j == 0:
            return terms[0][k]
        value = terms[1][k]
        for o in range(1, len(given)):
            value = jnp.where(given[o] == j, terms[1 + o][k], value)
        return value

    for off in range(band):
        value = None
        for j in range(entries):
            k = off - (entries - 1) + j
            if 0 <= k < entries:
                term = term_of(j, k)
                value = term if value is None else value + term
        rows[pl.ds(off, count, stride=8), :] = value
    shape = (8, slot_ref.shape[1])
    lines = lax.broadcasted_iota(jnp.int32, shape, 0) + position * band
    offs = lax.rem(lax.broadcasted_iota(jnp.int32, shape, 1), band).astype(jnp.float32)
    order = jnp.sum(jnp.where(slot_ref[...] == lines, offs, 0.0), axis=1, keepdims=True).astype(jnp.int32)
    order = jnp.broadcast_to(jnp.minimum(order, 7), (8, LANES))
    for c in range(count):
        placed = jnp.take_along_axis(rows[c * 8 : c * 8 + 8, :], order, axis=0, mode="promise_in_bounds")
        out_ref[:, c * LANES : (c + 1) * LANES] = placed[:band]


def per_device(three_index, coefficients, row_blocks, basis_blocks, fock_slot):
    entries, aux_count, block, depth = three_index.shape
    shard_rows, orbitals = coefficients.shape
    groups = lax.axis_size("aux")
    parts = lax.axis_size("occ")
    count = block * block // parts // LANES
    band = 2 * entries - 1

    def shift(value, axis, by):
        size = lax.axis_size(axis)
        return lax.ppermute(value, axis, [(i, (i + by) % size) for i in range(size)])

    def swap(value, first):
        pairs = [((i + first) % groups, (i + first + 1) % groups) for i in range(0, groups, 2)]
        return lax.ppermute(value, "aux", pairs + [(b, a) for a, b in pairs])

    other = shift(coefficients, "aux", -1)
    neighbour = shift(coefficients, "aux", 1)
    held = pl.pallas_call(
        fetch_kernel,
        out_shape=jax.ShapeDtypeStruct(three_index.shape, three_index.dtype),
        in_specs=[pl.BlockSpec(memory_space=pl.ANY)],
        out_specs=VMEM,
        scratch_shapes=[pltpu.SemaphoreType.DMA],
        compiler_params=pltpu.CompilerParams(vmem_limit_bytes=8 * 1024 * 1024),
    )(three_index)
    pieces = pl.pallas_call(
        functools.partial(build_kernel, groups, parts),
        out_shape=[jax.ShapeDtypeStruct((entries, entries, count, LANES), jnp.float32)] * parts,
        in_specs=[VMEM] * 5,
        out_specs=[VMEM] * parts,
        scratch_shapes=[
            pltpu.VMEM((3 * shard_rows, orbitals), jnp.bfloat16),
            pltpu.VMEM((entries // 2, 2 * depth, 2 * orbitals), jnp.bfloat16),
            pltpu.VMEM((entries * block, CHUNK * orbitals), jnp.bfloat16),
            pltpu.VMEM((entries * block, entries * block), jnp.float32),
            pltpu.VMEM((entries // 2, entries * block, LANES), jnp.float32),
        ],
        compiler_params=pltpu.CompilerParams(vmem_limit_bytes=12 * 1024 * 1024),
    )(basis_blocks.T, neighbour, coefficients, other, held)
    terms = [pieces[0]] + [shift(pieces[r], "occ", r) for r in range(1, parts)]
    targets, sends, takes = route(groups, entries)
    rows = pl.pallas_call(
        functools.partial(sum_kernel, parts, sends),
        out_shape=[jax.ShapeDtypeStruct((entries, count, LANES), jnp.float32)] * entries,
        in_specs=[VMEM] * parts,
        out_specs=[VMEM] * entries,
        compiler_params=pltpu.CompilerParams(vmem_limit_bytes=4 * 1024 * 1024),
    )(*terms)
    moved = [rows[0]]
    for value, each in zip(rows[1:], targets):
        moved.append(lax.ppermute(value, "aux", list(enumerate(each))))
    return pl.pallas_call(
        functools.partial(place_kernel, takes),
        out_shape=jax.ShapeDtypeStruct((band, count * LANES), jnp.float32),
        in_specs=[VMEM] * (entries + 1),
        out_specs=VMEM,
        scratch_shapes=[pltpu.VMEM((count * 8, LANES), jnp.float32)],
        compiler_params=pltpu.CompilerParams(vmem_limit_bytes=4 * 1024 * 1024),
    )(fock_slot.reshape(1, -1), *moved)


def solution(mesh):
    in_specs = (P("aux", None, None, None), P("aux", "occ"), P("aux"), P("aux", None), P())
    out_specs = P("aux", "occ")
    return jax.shard_map(
        per_device, mesh=mesh, in_specs=in_specs, out_specs=out_specs, check_vma=False
    )
```

```python
import functools

import jax
import jax.numpy as jnp
from jax import lax
from jax.experimental import pallas as pl
from jax.experimental.pallas import tpu as pltpu
from jax.sharding import PartitionSpec as P

LANES = 128
ROUTES = {
    16: [
        [8, 9, 10, 2, 12, 4, 5, 11, 7, 13, 14, 15, 0, 1, 6, 3],
        [4, 5, 6, 7, 8, 13, 10, 15, 0, 1, 9, 3, 11, 12, 2, 14],
        [15, 0, 1, 11, 3, 9, 14, 6, 12, 8, 2, 10, 4, 5, 13, 7],
    ],
}
CHUNK = 8
VMEM = pl.BlockSpec(memory_space=pltpu.VMEM)
SMEM = pl.BlockSpec(memory_space=pltpu.SMEM)


def fetch_kernel(source, target, sems):
    copies = [pltpu.make_async_copy(source.at[e], target.at[e], sems.at[e]) for e in range(source.shape[0])]
    for copy in copies:
        copy.start()
    for copy in copies:
        copy.wait()


def build_kernel(groups, parts, blocks_ref, near_ref, own_ref, far_ref, three_ref, *rest):
    outs, (near, sel, half, acc, panels) = rest[:parts], rest[parts:]
    entries, aux_count, block, depth = three_ref.shape
    tiles = depth // block
    shard_rows, orbitals = own_ref.shape
    per_shard = shard_rows // block
    position = lax.axis_index("aux")
    lane = lax.axis_index("occ")

    offset = lax.rem(blocks_ref[...] - (position - 1) * per_shard + groups * per_shard, groups * per_shard)
    side, within = lax.div(offset, per_shard), lax.rem(offset, per_shard)
    offsets = ((2 - side) * per_shard + within).astype(jnp.float32)
    tile_at = lax.broadcasted_iota(jnp.int32, offsets.shape, 0)
    entry_at = lax.broadcasted_iota(jnp.int32, offsets.shape, 1)

    near[0:shard_rows] = far_ref[...]
    near[shard_rows : 2 * shard_rows] = own_ref[...]
    near[2 * shard_rows : 3 * shard_rows] = near_ref[...]
    for pair in range(entries // 2):
        sel[pair] = jnp.zeros(sel.shape[1:], sel.dtype)
    for e in range(entries):
        for t in range(tiles):
            mine = (tile_at == t) & (entry_at == e)
            offset = jnp.max(jnp.where(mine, offsets, 0.0)).astype(jnp.int32) * block
            rows = near[pl.ds(pl.multiple_of(offset, block), block), :]
            at = (e % 2) * depth + t * block
            sel[e // 2, at : at + block, (e % 2) * orbitals : (e % 2 + 1) * orbitals] = rows

    acc[...] = jnp.zeros_like(acc)

    def step(s, carry):
        start = pl.multiple_of(s * CHUNK, CHUNK)
        for pair in range(entries // 2):
            lhs = jnp.concatenate(
                [three_ref[2 * pair + i, pl.ds(start, CHUNK)].reshape(CHUNK * block, depth) for i in range(2)], axis=1
            )
            res = jnp.dot(lhs, sel[pair], preferred_element_type=jnp.float32).astype(jnp.bfloat16)
            for i in range(2):
                e = 2 * pair + i
                for p in range(CHUNK):
                    half[e * block : (e + 1) * block, p * orbitals : (p + 1) * orbitals] = res[
                        p * block : (p + 1) * block, i * orbitals : (i + 1) * orbitals
                    ]
        full = half[...]
        acc[...] += lax.dot_general(full, full, (((1,), (1,)), ((), ())), preferred_element_type=jnp.float32)
        return carry

    lax.fori_loop(0, aux_count // CHUNK, step, 0, unroll=True)

    for h in range(entries // 2):
        panels[h] = acc[:, h * LANES : (h + 1) * LANES]
    count = block * block // parts // LANES
    low = lax.broadcasted_iota(jnp.int32, (count, LANES), 1) < block
    for r in range(parts):
        part = lax.rem(lane + r, parts)
        for j in range(entries):
            base = j * block + part * (block // parts)
            for k in range(0, entries, 2):
                even = panels[k // 2, pl.ds(base, count, stride=2), :]
                odd = panels[k // 2, pl.ds(base + 1, count, stride=2), :]
                outs[r][j, k] = jnp.where(low, even, pltpu.roll(odd, block, 1))
                outs[r][j, k + 1] = jnp.where(low, pltpu.roll(even, block, 1), odd)


def route(groups, entries):
    steps = [j * groups // entries for j in range(entries - 1)] + [groups - 1]
    targets = ROUTES.get(groups) or [[(i + step) % groups for i in range(groups)] for step in steps[1:]]
    sends = [[steps.index((t - i) % groups) for i, t in enumerate(each)] for each in targets]
    takes = [[sent[each.index(i)] for i in range(groups)] for each, sent in zip(targets, sends)]
    return targets, sends, takes


def entry_of(table, position):
    if len(set(table)) == 1:
        return table[0]
    packed = sum(value << (2 * i) for i, value in enumerate(table))
    packed = jnp.int32(packed - (1 << 32) if packed >= 1 << 31 else packed)
    return lax.shift_right_logical(packed, 2 * position) & 3


def sum_kernel(parts, sends, *refs):
    terms, outs = refs[:parts], refs[parts:]
    position = lax.axis_index("aux")
    for out, table in zip(outs, [[0]] + sends):
        j = entry_of(table, position)
        value = terms[0][j]
        for term in terms[1:]:
            value = value + term[j]
        out[...] = value


def place_kernel(takes, slot_ref, *refs):
    terms, out_ref, rows = refs[:-2], refs[-2], refs[-1]
    position = lax.axis_index("aux")
    entries, count = len(terms), terms[0].shape[1]
    band = 2 * entries - 1
    given = [entry_of(table, position) for table in takes]

    def term_of(j, k):
        if j == 0:
            return terms[0][k]
        value = terms[1][k]
        for o in range(1, len(given)):
            value = jnp.where(given[o] == j, terms[1 + o][k], value)
        return value

    for off in range(band):
        value = None
        for j in range(entries):
            k = off - (entries - 1) + j
            if 0 <= k < entries:
                term = term_of(j, k)
                value = term if value is None else value + term
        rows[pl.ds(off, count, stride=8), :] = value
    shape = (8, slot_ref.shape[1])
    lines = lax.broadcasted_iota(jnp.int32, shape, 0) + position * band
    offs = lax.rem(lax.broadcasted_iota(jnp.int32, shape, 1), band).astype(jnp.float32)
    order = jnp.sum(jnp.where(slot_ref[...] == lines, offs, 0.0), axis=1, keepdims=True).astype(jnp.int32)
    order = jnp.broadcast_to(jnp.minimum(order, 7), (8, LANES))
    for c in range(count):
        placed = jnp.take_along_axis(rows[c * 8 : c * 8 + 8, :], order, axis=0, mode="promise_in_bounds")
        out_ref[:, c * LANES : (c + 1) * LANES] = placed[:band]


def per_device(three_index, coefficients, row_blocks, basis_blocks, fock_slot):
    entries, aux_count, block, depth = three_index.shape
    shard_rows, orbitals = coefficients.shape
    groups = lax.axis_size("aux")
    parts = lax.axis_size("occ")
    count = block * block // parts // LANES
    band = 2 * entries - 1

    def shift(value, axis, by):
        size = lax.axis_size(axis)
        return lax.ppermute(value, axis, [(i, (i + by) % size) for i in range(size)])

    def swap(value, first):
        pairs = [((i + first) % groups, (i + first + 1) % groups) for i in range(0, groups, 2)]
        return lax.ppermute(value, "aux", pairs + [(b, a) for a, b in pairs])

    other = shift(coefficients, "aux", -1)
    neighbour = shift(coefficients, "aux", 1)
    held = pl.pallas_call(
        fetch_kernel,
        out_shape=jax.ShapeDtypeStruct(three_index.shape, three_index.dtype),
        in_specs=[pl.BlockSpec(memory_space=pl.ANY)],
        out_specs=VMEM,
        scratch_shapes=[pltpu.SemaphoreType.DMA((entries,))],
        compiler_params=pltpu.CompilerParams(vmem_limit_bytes=47 * 1024 * 1024),
    )(three_index)
    pieces = pl.pallas_call(
        functools.partial(build_kernel, groups, parts),
        out_shape=[jax.ShapeDtypeStruct((entries, entries, count, LANES), jnp.float32)] * parts,
        in_specs=[VMEM] * 5,
        out_specs=[VMEM] * parts,
        scratch_shapes=[
            pltpu.VMEM((3 * shard_rows, orbitals), jnp.bfloat16),
            pltpu.VMEM((entries // 2, 2 * depth, 2 * orbitals), jnp.bfloat16),
            pltpu.VMEM((entries * block, CHUNK * orbitals), jnp.bfloat16),
            pltpu.VMEM((entries * block, entries * block), jnp.float32),
            pltpu.VMEM((entries // 2, entries * block, LANES), jnp.float32),
        ],
        compiler_params=pltpu.CompilerParams(vmem_limit_bytes=12 * 1024 * 1024),
    )(basis_blocks.T, neighbour, coefficients, other, held)
    terms = [pieces[0]] + [shift(pieces[r], "occ", r) for r in range(1, parts)]
    targets, sends, takes = route(groups, entries)
    rows = pl.pallas_call(
        functools.partial(sum_kernel, parts, sends),
        out_shape=[jax.ShapeDtypeStruct((entries, count, LANES), jnp.float32)] * entries,
        in_specs=[VMEM] * parts,
        out_specs=[VMEM] * entries,
        compiler_params=pltpu.CompilerParams(vmem_limit_bytes=4 * 1024 * 1024),
    )(*terms)
    moved = [rows[0]]
    for value, each in zip(rows[1:], targets):
        moved.append(lax.ppermute(value, "aux", list(enumerate(each))))
    return pl.pallas_call(
        functools.partial(place_kernel, takes),
        out_shape=jax.ShapeDtypeStruct((band, count * LANES), jnp.float32),
        in_specs=[VMEM] * (entries + 1),
        out_specs=VMEM,
        scratch_shapes=[pltpu.VMEM((count * 8, LANES), jnp.float32)],
        compiler_params=pltpu.CompilerParams(vmem_limit_bytes=4 * 1024 * 1024),
    )(fock_slot.reshape(1, -1), *moved)


def solution(mesh):
    in_specs = (P("aux", None, None, None), P("aux", "occ"), P("aux"), P("aux", None), P())
    out_specs = P("aux", "occ")
    return jax.shard_map(
        per_device, mesh=mesh, in_specs=in_specs, out_specs=out_specs, check_vma=False
    )
```

```python
import functools

import jax
import jax.numpy as jnp
from jax import lax
from jax.experimental import pallas as pl
from jax.experimental.pallas import tpu as pltpu
from jax.sharding import PartitionSpec as P

LANES = 128
ROUTES = {
    16: [
        [8, 9, 10, 2, 12, 4, 5, 11, 7, 13, 14, 15, 0, 1, 6, 3],
        [4, 5, 6, 7, 8, 13, 10, 15, 0, 1, 9, 3, 11, 12, 2, 14],
        [15, 0, 1, 11, 3, 9, 14, 6, 12, 8, 2, 10, 4, 5, 13, 7],
    ],
}
CHUNK = 8
VMEM = pl.BlockSpec(memory_space=pltpu.VMEM)
SMEM = pl.BlockSpec(memory_space=pltpu.SMEM)


def fetch_kernel(source, target, sems):
    copies = [pltpu.make_async_copy(source.at[e], target.at[e], sems.at[e]) for e in range(source.shape[0])]
    for copy in copies:
        copy.start()
    for copy in copies:
        copy.wait()


def build_kernel(groups, parts, blocks_ref, near_ref, own_ref, far_ref, three_ref, *rest):
    outs, firsts, (near, sel, half, acc, panels) = rest[:parts], rest[parts : 2 * parts], rest[2 * parts :]
    entries, aux_count, block, depth = three_ref.shape
    tiles = depth // block
    shard_rows, orbitals = own_ref.shape
    per_shard = shard_rows // block
    position = lax.axis_index("aux")
    lane = lax.axis_index("occ")

    offset = lax.rem(blocks_ref[...] - (position - 1) * per_shard + groups * per_shard, groups * per_shard)
    side, within = lax.div(offset, per_shard), lax.rem(offset, per_shard)
    offsets = ((2 - side) * per_shard + within).astype(jnp.float32)
    tile_at = lax.broadcasted_iota(jnp.int32, offsets.shape, 0)
    entry_at = lax.broadcasted_iota(jnp.int32, offsets.shape, 1)

    near[0:shard_rows] = far_ref[...]
    near[shard_rows : 2 * shard_rows] = own_ref[...]
    near[2 * shard_rows : 3 * shard_rows] = near_ref[...]
    for pair in range(entries // 2):
        sel[pair] = jnp.zeros(sel.shape[1:], sel.dtype)
    for e in range(entries):
        for t in range(tiles):
            mine = (tile_at == t) & (entry_at == e)
            offset = jnp.max(jnp.where(mine, offsets, 0.0)).astype(jnp.int32) * block
            rows = near[pl.ds(pl.multiple_of(offset, block), block), :]
            at = (e % 2) * depth + t * block
            sel[e // 2, at : at + block, (e % 2) * orbitals : (e % 2 + 1) * orbitals] = rows

    acc[...] = jnp.zeros_like(acc)

    def step(s, carry):
        start = pl.multiple_of(s * CHUNK, CHUNK)
        for pair in range(entries // 2):
            lhs = jnp.concatenate(
                [three_ref[2 * pair + i, pl.ds(start, CHUNK)].reshape(CHUNK * block, depth) for i in range(2)], axis=1
            )
            res = jnp.dot(lhs, sel[pair], preferred_element_type=jnp.float32).astype(jnp.bfloat16)
            for i in range(2):
                e = 2 * pair + i
                for p in range(CHUNK):
                    half[e * block : (e + 1) * block, p * orbitals : (p + 1) * orbitals] = res[
                        p * block : (p + 1) * block, i * orbitals : (i + 1) * orbitals
                    ]
        full = half[...]
        acc[...] += lax.dot_general(full, full, (((1,), (1,)), ((), ())), preferred_element_type=jnp.float32)
        return carry

    lax.fori_loop(0, aux_count // CHUNK, step, 0, unroll=True)

    for h in range(entries // 2):
        panels[h] = acc[:, h * LANES : (h + 1) * LANES]
    count = block * block // parts // LANES
    low = lax.broadcasted_iota(jnp.int32, (count, LANES), 1) < block
    for r in range(parts):
        part = lax.rem(lane + r, parts)
        for j in range(entries):
            base = j * block + part * (block // parts)
            for k in range(0, entries, 2):
                even = panels[k // 2, pl.ds(base, count, stride=2), :]
                odd = panels[k // 2, pl.ds(base + 1, count, stride=2), :]
                out = firsts[r] if j == 0 else outs[r].at[j - 1]
                out[k] = jnp.where(low, even, pltpu.roll(odd, block, 1))
                out[k + 1] = jnp.where(low, pltpu.roll(even, block, 1), odd)


def route(groups, entries):
    steps = [j * groups // entries for j in range(entries - 1)] + [groups - 1]
    targets = ROUTES.get(groups) or [[(i + step) % groups for i in range(groups)] for step in steps[1:]]
    sends = [[steps.index((t - i) % groups) for i, t in enumerate(each)] for each in targets]
    takes = [[sent[each.index(i)] for i in range(groups)] for each, sent in zip(targets, sends)]
    return targets, sends, takes


def entry_of(table, position):
    if len(set(table)) == 1:
        return table[0]
    packed = sum(value << (2 * i) for i, value in enumerate(table))
    packed = jnp.int32(packed - (1 << 32) if packed >= 1 << 31 else packed)
    return lax.shift_right_logical(packed, 2 * position) & 3


def sum_kernel(parts, sends, *refs):
    terms, outs = refs[:parts], refs[parts:]
    position = lax.axis_index("aux")
    for out, table in zip(outs, sends):
        j = entry_of(table, position)
        value = terms[0][j - 1]
        for term in terms[1:]:
            value = value + term[j - 1]
        out[...] = value


def place_kernel(parts, takes, slot_ref, *refs):
    firsts, terms, out_ref, rows = refs[:parts], refs[parts:-2], refs[-2], refs[-1]
    position = lax.axis_index("aux")
    entries, count = firsts[0].shape[:2]
    band = 2 * entries - 1
    given = [entry_of(table, position) for table in takes]

    def term_of(j, k):
        if j == 0:
            return sum((first[k] for first in firsts[1:]), firsts[0][k])
        value = terms[0][k]
        for o in range(1, len(given)):
            value = jnp.where(given[o] == j, terms[o][k], value)
        return value

    for off in range(band):
        value = None
        for j in range(entries):
            k = off - (entries - 1) + j
            if 0 <= k < entries:
                term = term_of(j, k)
                value = term if value is None else value + term
        rows[pl.ds(off, count, stride=8), :] = value
    shape = (8, slot_ref.shape[1])
    lines = lax.broadcasted_iota(jnp.int32, shape, 0) + position * band
    offs = lax.rem(lax.broadcasted_iota(jnp.int32, shape, 1), band).astype(jnp.float32)
    order = jnp.sum(jnp.where(slot_ref[...] == lines, offs, 0.0), axis=1, keepdims=True).astype(jnp.int32)
    order = jnp.broadcast_to(jnp.minimum(order, 7), (8, LANES))
    for c in range(count):
        placed = jnp.take_along_axis(rows[c * 8 : c * 8 + 8, :], order, axis=0, mode="promise_in_bounds")
        out_ref[:, c * LANES : (c + 1) * LANES] = placed[:band]


def per_device(three_index, coefficients, row_blocks, basis_blocks, fock_slot):
    entries, aux_count, block, depth = three_index.shape
    shard_rows, orbitals = coefficients.shape
    groups = lax.axis_size("aux")
    parts = lax.axis_size("occ")
    count = block * block // parts // LANES
    band = 2 * entries - 1

    def shift(value, axis, by):
        size = lax.axis_size(axis)
        return lax.ppermute(value, axis, [(i, (i + by) % size) for i in range(size)])

    def swap(value, first):
        pairs = [((i + first) % groups, (i + first + 1) % groups) for i in range(0, groups, 2)]
        return lax.ppermute(value, "aux", pairs + [(b, a) for a, b in pairs])

    other = shift(coefficients, "aux", -1)
    neighbour = shift(coefficients, "aux", 1)
    held = pl.pallas_call(
        fetch_kernel,
        out_shape=jax.ShapeDtypeStruct(three_index.shape, three_index.dtype),
        in_specs=[pl.BlockSpec(memory_space=pl.ANY)],
        out_specs=VMEM,
        scratch_shapes=[pltpu.SemaphoreType.DMA((entries,))],
        compiler_params=pltpu.CompilerParams(vmem_limit_bytes=47 * 1024 * 1024),
    )(three_index)
    pieces = pl.pallas_call(
        functools.partial(build_kernel, groups, parts),
        out_shape=[jax.ShapeDtypeStruct((entries - 1, entries, count, LANES), jnp.float32)] * parts
        + [jax.ShapeDtypeStruct((entries, count, LANES), jnp.float32)] * parts,
        in_specs=[VMEM] * 5,
        out_specs=[VMEM] * (2 * parts),
        scratch_shapes=[
            pltpu.VMEM((3 * shard_rows, orbitals), jnp.bfloat16),
            pltpu.VMEM((entries // 2, 2 * depth, 2 * orbitals), jnp.bfloat16),
            pltpu.VMEM((entries * block, CHUNK * orbitals), jnp.bfloat16),
            pltpu.VMEM((entries * block, entries * block), jnp.float32),
            pltpu.VMEM((entries // 2, entries * block, LANES), jnp.float32),
        ],
        compiler_params=pltpu.CompilerParams(vmem_limit_bytes=12 * 1024 * 1024),
    )(basis_blocks.T, neighbour, coefficients, other, held)
    terms = [pieces[0]] + [shift(pieces[r], "occ", r) for r in range(1, parts)]
    targets, sends, takes = route(groups, entries)
    rows = pl.pallas_call(
        functools.partial(sum_kernel, parts, sends),
        out_shape=[jax.ShapeDtypeStruct((entries, count, LANES), jnp.float32)] * (entries - 1),
        in_specs=[VMEM] * parts,
        out_specs=[VMEM] * (entries - 1),
        compiler_params=pltpu.CompilerParams(vmem_limit_bytes=4 * 1024 * 1024),
    )(*terms)
    moved = []
    for value, each in zip(rows, targets):
        moved.append(lax.ppermute(value, "aux", list(enumerate(each))))
    firsts = [pieces[parts]] + [shift(pieces[parts + r], "occ", r) for r in range(1, parts)]
    return pl.pallas_call(
        functools.partial(place_kernel, parts, takes),
        out_shape=jax.ShapeDtypeStruct((band, count * LANES), jnp.float32),
        in_specs=[VMEM] * (entries + parts),
        out_specs=VMEM,
        scratch_shapes=[pltpu.VMEM((count * 8, LANES), jnp.float32)],
        compiler_params=pltpu.CompilerParams(vmem_limit_bytes=4 * 1024 * 1024),
    )(fock_slot.reshape(1, -1), *firsts, *moved)


def solution(mesh):
    in_specs = (P("aux", None, None, None), P("aux", "occ"), P("aux"), P("aux", None), P())
    out_specs = P("aux", "occ")
    return jax.shard_map(
        per_device, mesh=mesh, in_specs=in_specs, out_specs=out_specs, check_vma=False
    )
```

```python
import functools

import jax
import jax.numpy as jnp
from jax import lax
from jax.experimental import pallas as pl
from jax.experimental.pallas import tpu as pltpu
from jax.sharding import PartitionSpec as P

LANES = 128
ROUTES = {
    16: [
        [8, 9, 10, 2, 12, 4, 5, 11, 7, 13, 14, 15, 0, 1, 6, 3],
        [4, 5, 6, 7, 8, 13, 10, 15, 0, 1, 9, 3, 11, 12, 2, 14],
        [15, 0, 1, 11, 3, 9, 14, 6, 12, 8, 2, 10, 4, 5, 13, 7],
    ],
}
SLOTS = 8
CHUNK = 8
VMEM = pl.BlockSpec(memory_space=pltpu.VMEM)
SMEM = pl.BlockSpec(memory_space=pltpu.SMEM)


def fetch_kernel(source, target, sems):
    copies = [pltpu.make_async_copy(source.at[e], target.at[e], sems.at[e]) for e in range(source.shape[0])]
    for copy in copies:
        copy.start()
    for copy in copies:
        copy.wait()


def build_kernel(groups, parts, blocks_ref, near_ref, own_ref, far_ref, three_ref, *rest):
    outs, firsts, (near, sel, half, acc, panels) = rest[:parts], rest[parts : 2 * parts], rest[2 * parts :]
    entries, aux_count, block, depth = three_ref.shape
    tiles = depth // block
    shard_rows, orbitals = own_ref.shape
    per_shard = shard_rows // block
    position = lax.axis_index("aux")
    lane = lax.axis_index("occ")

    offset = lax.rem(blocks_ref[...] - (position - 1) * per_shard + groups * per_shard, groups * per_shard)
    side, within = lax.div(offset, per_shard), lax.rem(offset, per_shard)
    offsets = ((2 - side) * per_shard + within).astype(jnp.float32)
    tile_at = lax.broadcasted_iota(jnp.int32, offsets.shape, 0)
    entry_at = lax.broadcasted_iota(jnp.int32, offsets.shape, 1)

    near[0:shard_rows] = far_ref[...]
    near[shard_rows : 2 * shard_rows] = own_ref[...]
    near[2 * shard_rows : 3 * shard_rows] = near_ref[...]
    for pair in range(entries // 2):
        sel[pair] = jnp.zeros(sel.shape[1:], sel.dtype)
    for e in range(entries):
        for t in range(tiles):
            mine = (tile_at == t) & (entry_at == e)
            offset = jnp.max(jnp.where(mine, offsets, 0.0)).astype(jnp.int32) * block
            rows = near[pl.ds(pl.multiple_of(offset, block), block), :]
            at = (e % 2) * depth + t * block
            sel[e // 2, at : at + block, (e % 2) * orbitals : (e % 2 + 1) * orbitals] = rows

    def transform(s):
        for pair in range(entries // 2):
            lhs = jnp.concatenate(
                [
                    three_ref[2 * pair + i, s * CHUNK : (s + 1) * CHUNK].reshape(CHUNK * block, depth)
                    for i in range(2)
                ],
                axis=1,
            )
            res = jnp.dot(lhs, sel[pair], preferred_element_type=jnp.float32).astype(jnp.bfloat16)
            for i in range(2):
                e = 2 * pair + i
                for p in range(CHUNK):
                    half[s % SLOTS, e * block : (e + 1) * block, p * orbitals : (p + 1) * orbitals] = res[
                        p * block : (p + 1) * block, i * orbitals : (i + 1) * orbitals
                    ]

    def gather(s):
        full = half[s % SLOTS]
        value = lax.dot_general(full, full, (((1,), (1,)), ((), ())), preferred_element_type=jnp.float32)
        if s == 0:
            acc[...] = value
        elif s < aux_count // CHUNK - 1:
            acc[...] += value
        else:
            value = acc[...] + value
            for h in range(entries // 2):
                panels[h] = value[:, h * LANES : (h + 1) * LANES]

    transform(0)
    for s in range(1, aux_count // CHUNK):
        transform(s)
        gather(s - 1)
    gather(aux_count // CHUNK - 1)

    count = block * block // parts // LANES
    low = lax.broadcasted_iota(jnp.int32, (count, LANES), 1) < block
    for r in range(parts):
        part = lax.rem(lane + r, parts)
        for j in range(entries):
            base = j * block + part * (block // parts)
            for k in range(0, entries, 2):
                even = panels[k // 2, pl.ds(base, count, stride=2), :]
                odd = panels[k // 2, pl.ds(base + 1, count, stride=2), :]
                out = firsts[r] if j == 0 else outs[r].at[j - 1]
                out[k] = jnp.where(low, even, pltpu.roll(odd, block, 1))
                out[k + 1] = jnp.where(low, pltpu.roll(even, block, 1), odd)


def route(groups, entries):
    steps = [j * groups // entries for j in range(entries - 1)] + [groups - 1]
    targets = ROUTES.get(groups) or [[(i + step) % groups for i in range(groups)] for step in steps[1:]]
    sends = [[steps.index((t - i) % groups) for i, t in enumerate(each)] for each in targets]
    takes = [[sent[each.index(i)] for i in range(groups)] for each, sent in zip(targets, sends)]
    return targets, sends, takes


def entry_of(table, position):
    if len(set(table)) == 1:
        return table[0]
    packed = sum(value << (2 * i) for i, value in enumerate(table))
    packed = jnp.int32(packed - (1 << 32) if packed >= 1 << 31 else packed)
    return lax.shift_right_logical(packed, 2 * position) & 3


def sum_kernel(parts, sends, *refs):
    terms, outs = refs[:parts], refs[parts:]
    position = lax.axis_index("aux")
    for out, table in zip(outs, sends):
        j = entry_of(table, position)
        value = terms[0][j - 1]
        for term in terms[1:]:
            value = value + term[j - 1]
        out[...] = value


def place_kernel(parts, takes, slot_ref, *refs):
    firsts, terms, out_ref, rows = refs[:parts], refs[parts:-2], refs[-2], refs[-1]
    position = lax.axis_index("aux")
    entries, count = firsts[0].shape[:2]
    band = 2 * entries - 1
    given = [entry_of(table, position) for table in takes]

    def term_of(j, k):
        if j == 0:
            return sum((first[k] for first in firsts[1:]), firsts[0][k])
        value = terms[0][k]
        for o in range(1, len(given)):
            value = jnp.where(given[o] == j, terms[o][k], value)
        return value

    for off in range(band):
        value = None
        for j in range(entries):
            k = off - (entries - 1) + j
            if 0 <= k < entries:
                term = term_of(j, k)
                value = term if value is None else value + term
        rows[pl.ds(off, count, stride=8), :] = value
    shape = (8, slot_ref.shape[1])
    lines = lax.broadcasted_iota(jnp.int32, shape, 0) + position * band
    offs = lax.rem(lax.broadcasted_iota(jnp.int32, shape, 1), band).astype(jnp.float32)
    order = jnp.sum(jnp.where(slot_ref[...] == lines, offs, 0.0), axis=1, keepdims=True).astype(jnp.int32)
    order = jnp.broadcast_to(jnp.minimum(order, 7), (8, LANES))
    for c in range(count):
        placed = jnp.take_along_axis(rows[c * 8 : c * 8 + 8, :], order, axis=0, mode="promise_in_bounds")
        out_ref[:, c * LANES : (c + 1) * LANES] = placed[:band]


def per_device(three_index, coefficients, row_blocks, basis_blocks, fock_slot):
    entries, aux_count, block, depth = three_index.shape
    shard_rows, orbitals = coefficients.shape
    groups = lax.axis_size("aux")
    parts = lax.axis_size("occ")
    count = block * block // parts // LANES
    band = 2 * entries - 1

    def shift(value, axis, by):
        size = lax.axis_size(axis)
        return lax.ppermute(value, axis, [(i, (i + by) % size) for i in range(size)])

    def swap(value, first):
        pairs = [((i + first) % groups, (i + first + 1) % groups) for i in range(0, groups, 2)]
        return lax.ppermute(value, "aux", pairs + [(b, a) for a, b in pairs])

    other = shift(coefficients, "aux", -1)
    neighbour = shift(coefficients, "aux", 1)
    held = pl.pallas_call(
        fetch_kernel,
        out_shape=jax.ShapeDtypeStruct(three_index.shape, three_index.dtype),
        in_specs=[pl.BlockSpec(memory_space=pl.ANY)],
        out_specs=VMEM,
        scratch_shapes=[pltpu.SemaphoreType.DMA((entries,))],
        compiler_params=pltpu.CompilerParams(vmem_limit_bytes=47 * 1024 * 1024),
    )(three_index)
    pieces = pl.pallas_call(
        functools.partial(build_kernel, groups, parts),
        out_shape=[jax.ShapeDtypeStruct((entries - 1, entries, count, LANES), jnp.float32)] * parts
        + [jax.ShapeDtypeStruct((entries, count, LANES), jnp.float32)] * parts,
        in_specs=[VMEM] * 5,
        out_specs=[VMEM] * (2 * parts),
        scratch_shapes=[
            pltpu.VMEM((3 * shard_rows, orbitals), jnp.bfloat16),
            pltpu.VMEM((entries // 2, 2 * depth, 2 * orbitals), jnp.bfloat16),
            pltpu.VMEM((SLOTS, entries * block, CHUNK * orbitals), jnp.bfloat16),
            pltpu.VMEM((entries * block, entries * block), jnp.float32),
            pltpu.VMEM((entries // 2, entries * block, LANES), jnp.float32),
        ],
        compiler_params=pltpu.CompilerParams(vmem_limit_bytes=16 * 1024 * 1024),
    )(basis_blocks.T, neighbour, coefficients, other, held)
    terms = [pieces[0]] + [shift(pieces[r], "occ", r) for r in range(1, parts)]
    targets, sends, takes = route(groups, entries)
    rows = pl.pallas_call(
        functools.partial(sum_kernel, parts, sends),
        out_shape=[jax.ShapeDtypeStruct((entries, count, LANES), jnp.float32)] * (entries - 1),
        in_specs=[VMEM] * parts,
        out_specs=[VMEM] * (entries - 1),
        compiler_params=pltpu.CompilerParams(vmem_limit_bytes=4 * 1024 * 1024),
    )(*terms)
    moved = []
    for value, each in zip(rows, targets):
        moved.append(lax.ppermute(value, "aux", list(enumerate(each))))
    firsts = [pieces[parts]] + [shift(pieces[parts + r], "occ", r) for r in range(1, parts)]
    return pl.pallas_call(
        functools.partial(place_kernel, parts, takes),
        out_shape=jax.ShapeDtypeStruct((band, count * LANES), jnp.float32),
        in_specs=[VMEM] * (entries + parts),
        out_specs=VMEM,
        scratch_shapes=[pltpu.VMEM((count * 8, LANES), jnp.float32)],
        compiler_params=pltpu.CompilerParams(vmem_limit_bytes=4 * 1024 * 1024),
    )(fock_slot.reshape(1, -1), *firsts, *moved)


def solution(mesh):
    in_specs = (P("aux", None, None, None), P("aux", "occ"), P("aux"), P("aux", None), P())
    out_specs = P("aux", "occ")
    return jax.shard_map(
        per_device, mesh=mesh, in_specs=in_specs, out_specs=out_specs, check_vma=False
    )
```
